128 devices in a mesh: rows: 16 (over y, z), feat: 8 (over x, core).
Axes of the slice: x: 4, y: 4, z: 4, core: 2. Of those that a mesh axis runs over, the one named last changes fastest.
Arguments:
- features: bfloat16 [32768, 1024], P('rows', 'feat'), may hold values from -6 to 6
- tiles: bfloat16 [10240, 128, 128], P('rows'), may hold values from -0.078125 to 0.078125
- tile_row: int32 [10240], P('rows'), may hold values from 0 to 15, as said below
- tile_panel: int32 [10240], P('rows'), may hold values from 0 to 15
- tile_slot: int32 [10240], P('rows'), may hold values from 0 to 7
- counts: int32 [16], P('rows'), may hold values from 1 to 640, as said below
- need_list: int32 [16, 16, 8], replicated, may hold values from 0 to 15, as said below
- weight: bfloat16 [1024, 1024], replicated, may hold values from -0.1875 to 0.1875
Outputs:
- activations: bfloat16 [32768, 1024], P(('rows', 'feat'))
The draws below stay inside these ranges and needn't reach their ends.
Inputs may be any that keep to these rules, and one draw needn't show every extreme that they name: need_list[g, p] holds 8 distinct tile rows of panel p. Within a row group the slots name distinct (tile_row, tile_panel, tile_slot) triples. `counts`: some row group lists exactly 640 tiles.
All inputs are finite; a program needn't handle non-finite values.
Results may differ from the reference program's by a relative error of at most 0.0049.
Values may be sent and summed in bfloat16 or wider, within the bound.
A program may use at most 128 MiB of HBM per device.

```python
import jax
import jax.numpy as jnp
from jax import lax

H = 1024
TILE = 128
TPP = 16
MAXT = 640
NEED = 8
VG = 2048
GROUPS = 16
V = 32768


def layout(key):
    keys = jax.random.split(jax.random.fold_in(key, 7), 4)
    need_scores = jax.random.randint(keys[0], (GROUPS, GROUPS, TPP), 0, 65536) * TPP + jnp.arange(TPP, dtype=jnp.int32)
    need_values, need_index = lax.top_k(need_scores, NEED)
    combos = TPP * GROUPS * NEED
    pick_scores = jax.random.randint(keys[1], (GROUPS, combos), 0, 65536) * combos + jnp.arange(combos, dtype=jnp.int32)
    pick_values, picked = lax.top_k(pick_scores, MAXT)
    row_ids = picked // (GROUPS * NEED)
    panel_ids = picked // NEED % GROUPS
    slot_ids = picked % NEED
    base_counts = jax.random.randint(keys[2], (GROUPS,), max(1, MAXT // 8), MAXT // 2 + 1)
    heavy = jax.random.randint(keys[3], (), 0, GROUPS)
    group_counts = jnp.where(jnp.arange(GROUPS, dtype=jnp.int32) == heavy, MAXT, base_counts)
    return (need_index.astype(jnp.int32), row_ids.reshape(-1).astype(jnp.int32), panel_ids.reshape(-1).astype(jnp.int32), slot_ids.reshape(-1).astype(jnp.int32), group_counts.astype(jnp.int32))


def draw_need_list(key, part):
    return layout(key)[0]


def draw_tile_row(key, part):
    return layout(key)[1]


def draw_tile_panel(key, part):
    return layout(key)[2]


def draw_tile_slot(key, part):
    return layout(key)[3]


def draw_counts(key, part):
    return layout(key)[4]


def block_levels(own_key, extent, cuts, smallest, largest):
    loudness = 1.0
    for dim, shards_of in cuts:
        steps = jax.random.uniform(jax.random.fold_in(jax.random.fold_in(own_key, 6), dim), (shards_of,), jnp.float32, smallest / len(cuts), largest / len(cuts))
        loudness = loudness * jnp.repeat(jnp.exp(steps), extent[dim] // shards_of).reshape((-1,) + (1,) * (len(extent) - 1 - dim))
    return loudness


def scatter_about(own_key, shape, spread, limit, cuts=(), kind=jnp.bfloat16):
    values = jax.random.normal(own_key, shape, jnp.float32) * spread
    if len(cuts) > 0:
        values = block_levels(own_key, shape, cuts, -0.22, 0.18) * values
    return jnp.clip(values, min=-limit, max=limit).astype(kind)


def setup_inputs(seed: int = 0) -> dict:
    seeds = jax.random.split(jax.random.key(seed), 9)
    features = scatter_about(seeds[0], (V, H), 1.0, 6.0, ((0, 16), (1, 8)))
    tiles = scatter_about(seeds[1], (GROUPS * MAXT, TILE, TILE), (TILE * MAXT // TPP) ** -0.5, 0.078125, ((0, 16),))
    tile_row = draw_tile_row(jax.random.fold_in(seeds[8], 71), 0)
    tile_panel = draw_tile_panel(jax.random.fold_in(seeds[8], 71), 0)
    tile_slot = draw_tile_slot(jax.random.fold_in(seeds[8], 71), 0)
    counts = draw_counts(jax.random.fold_in(seeds[8], 71), 0)
    need_list = draw_need_list(jax.random.fold_in(seeds[8], 71), 0)
    weight = scatter_about(seeds[7], (H, H), H ** -0.5, 0.1875)
    return {"features": features, "tiles": tiles, "tile_row": tile_row, "tile_panel": tile_panel, "tile_slot": tile_slot, "counts": counts, "need_list": need_list, "weight": weight}


def reference(features, tiles, tile_row, tile_panel, tile_slot, counts, need_list, weight):
    blocks = features.reshape(GROUPS * TPP, TILE, H)

    def group_rows(group):
        first_slot = group * MAXT
        tile_group = lax.dynamic_slice_in_dim(tiles, first_slot, MAXT, 0).astype(jnp.float32)
        row_ids = lax.dynamic_slice_in_dim(tile_row, first_slot, MAXT, 0)
        panel_ids = lax.dynamic_slice_in_dim(tile_panel, first_slot, MAXT, 0)
        slot_ids = lax.dynamic_slice_in_dim(tile_slot, first_slot, MAXT, 0)
        table = need_list[group]
        block_ids = (panel_ids * TPP + table[panel_ids, slot_ids]).astype(jnp.int32)
        fetched = blocks[block_ids].astype(jnp.float32)
        product = jnp.einsum("sij,sjh->sih", tile_group, fetched, precision=lax.Precision.HIGHEST)
        live_slot = (jnp.arange(MAXT, dtype=jnp.int32) < counts[group]).astype(product.dtype)
        product = product * live_slot[:, None, None]
        return jax.ops.segment_sum(product, row_ids, num_segments=TPP)

    summed = lax.map(group_rows, jnp.arange(GROUPS, dtype=jnp.int32))
    rounded = summed.reshape(GROUPS * VG, H).astype(jnp.bfloat16)
    mixed = jnp.dot(rounded, weight, preferred_element_type=jnp.float32)
    return jnp.maximum(mixed, 0.0).astype(jnp.bfloat16)
```

```python
import functools

import jax
import jax.numpy as jnp
from jax import lax
from jax.experimental import pallas as pl
from jax.experimental.pallas import tpu as pltpu
from jax.sharding import PartitionSpec as P

TILE = 128
TPP = 16
NEED = 8
GROUPS = 16
FEAT = 8
MAXT = 640
CHUNKS = 4
PER = TPP // CHUNKS
TILE_DMAS = 8
MESH = pl.DeviceIdType.MESH

INNER = {4: (0, 2), 8: (0, 3), 6: (4, 1), 9: (8, 0), 11: (9, 1)}
LEAF = {1: (0, 0), 2: (0, 1), 10: (8, 1), 12: (8, 2), 5: (4, 0), 13: (9, 2), 7: (6, 0), 14: (6, 3), 3: (11, 3), 15: (11, 2)}
INNER_LIST = [4, 8, 6, 9, 11]
LEAF_LIST = list(LEAF)
HELD = [0] + INNER_LIST
ORDER = [0, 8, 4, 9, 6, 1, 12, 11, 2, 10, 5, 13, 7, 14, 3, 15]
CHILD = {4: [6], 8: [9], 9: [11]}

BEFORE = [
    ("in", 8, 0), ("in", 4, 0), ("in", 8, 1), ("in", 4, 1), ("in", 8, 2), ("in", 9, 0), ("in", 8, 3), ("in", 4, 2),
]
STEPS = {
    0: [("use", 0)],
    1: [("use", 8), ("in", 9, 1)],
    2: [("in", 4, 3), ("in", 9, 2), ("use", 4), ("send", 1), ("send", 12)],
    3: [("in", 9, 3), ("use", 9), ("send", 5), ("send", 13)],
    4: [("in", 6, 0), ("in", 6, 1), ("in", 6, 2), ("in", 6, 3), ("use", 6), ("send", 2), ("send", 10), ("send", 7), ("send", 14)],
    5: [("get", 1)],
    6: [("get", 12)],
    7: [("in", 11, 0), ("in", 11, 1), ("in", 11, 2), ("in", 11, 3), ("use", 11), ("send", 3), ("send", 15)],
    8: [("get", 2)],
    9: [("get", 10)],
    10: [("get", 5)],
    11: [("get", 13)],
    12: [("get", 7)],
    13: [("get", 14)],
    14: [("get", 3)],
    15: [("get", 15)],
}


def flip(c, bits):
    return (c, c + 1 - 2 * (c % 2), 3 - c, (c + 2) % 4)[bits]


def layer_kernel(features, tiles, row_hbm, panel_hbm, slot_hbm, count_hbm, need_hbm, weight, out,
                 held0, held1, held2, held3, held4, held5, parts, outbox, tile_mem, table_vec, table, row_mem, panel_mem,
                 slot_mem, count_mem, need_mem, panel_of, total, weight_mem, mail, inbox,
                 local_sem, tile_sem, small_sem, inner_send, inner_recv, leaf_send, leaf_recv, mail_send, mail_recv):
    group, member = lax.axis_index("rows"), lax.axis_index("feat")
    core = member % 2
    y, z = group // 4, group % 4
    first, second = y + core * (z - y), z + core * (y - z)
    held = dict(zip(HELD, (held0, held1, held2, held3, held4, held5)))

    def group_at(v):
        a, b = flip(first, v & 3), flip(second, v >> 2)
        return (a + core * (b - a)) * 4 + b + core * (a - b)

    own_copy = pltpu.make_async_copy(features, held0, local_sem.at[0])
    own_copy.start()
    small = [
        pltpu.make_async_copy(row_hbm, row_mem, small_sem.at[0]),
        pltpu.make_async_copy(panel_hbm, panel_mem, small_sem.at[1]),
        pltpu.make_async_copy(slot_hbm, slot_mem, small_sem.at[2]),
        pltpu.make_async_copy(count_hbm, count_mem, small_sem.at[3]),
        pltpu.make_async_copy(need_hbm.at[group], need_mem.at[0], small_sem.at[4]),
    ] + [
        pltpu.make_async_copy(need_hbm.at[group_at(1 << d)], need_mem.at[1 + d], small_sem.at[5 + d]) for d in range(4)
    ]
    for copy in small:
        copy.start()

    barrier = pltpu.get_barrier_semaphore()
    for d in range(4):
        pl.semaphore_signal(barrier, inc=1, device_id=(group_at(1 << d), member), device_id_type=MESH)
    for step in range(1, FEAT):
        pl.semaphore_signal(barrier, inc=1, device_id=(group, (member + step) % FEAT), device_id_type=MESH)

    share = MAXT // TILE_DMAS
    tile_copies = [
        pltpu.make_async_copy(tiles.at[pl.ds(i * share, share)], tile_mem.at[pl.ds(i * share, share)], tile_sem.at[i])
        for i in range(TILE_DMAS)
    ]
    weight_copy = pltpu.make_async_copy(weight, weight_mem, local_sem.at[1])

    def inner_copy(w, c):
        v, d = INNER[w]
        i = INNER_LIST.index(w) * CHUNKS + c
        rows = pl.ds(c * PER, PER)
        return pltpu.make_async_remote_copy(
            src_ref=held[v].at[rows], dst_ref=held[w].at[rows], send_sem=inner_send.at[i], recv_sem=inner_recv.at[i],
            device_id=(group_at(1 << d), member), device_id_type=MESH)

    def leaf_copy(w):
        d = LEAF[w][1]
        i = LEAF_LIST.index(w)
        return pltpu.make_async_remote_copy(
            src_ref=outbox.at[i], dst_ref=parts.at[ORDER.index(w)], send_sem=leaf_send.at[i], recv_sem=leaf_recv.at[i],
            device_id=(group_at(1 << d), member), device_id_type=MESH)

    def perform(event):
        kind, v = event[0], event[1]
        if kind == "in":
            inner_copy(v, event[2]).wait_recv()
            for w in CHILD.get(v, []):
                inner_copy(w, event[2]).start()
        elif kind == "use":
            k, panel = ORDER.index(v), group_at(v)
            for s in range(NEED):
                parts[k, s] = held[v][need_mem[0, panel, s]]
        elif kind == "send":
            u, d = LEAF[v]
            i, panel = LEAF_LIST.index(v), group_at(u)
            for s in range(NEED):
                outbox[i, s] = held[u][need_mem[1 + d, panel, s]]
            leaf_copy(v).start()
        else:
            leaf_copy(v).wait_recv()

    own_copy.wait()
    pl.semaphore_wait(barrier, 4 + FEAT - 1)
    for c in range(CHUNKS):
        inner_copy(8, c).start()
        inner_copy(4, c).start()
    for copy in tile_copies:
        copy.start()
    weight_copy.start()
    for copy in small:
        copy.wait()

    for k, v in enumerate(ORDER):
        panel_of[k] = group_at(v)
    count = count_mem[0]
    place = lax.broadcasted_iota(jnp.int32, (TPP, TILE), 0) * TILE + lax.broadcasted_iota(jnp.int32, (TPP, TILE), 1)

    def enter(k, found):
        code = row_mem[k] * TILE + panel_mem[k] * NEED + slot_mem[k]
        code = jnp.where(k < count, code, -1)
        return jnp.where(place == code, k, found)

    table_vec[...] = lax.fori_loop(0, MAXT, enter, jnp.full((TPP, TILE), MAXT, jnp.int32), unroll=8)
    table_copy = pltpu.make_async_copy(table_vec, table, local_sem.at[2])
    table_copy.start()
    tile_mem[MAXT] = jnp.zeros((TILE, TILE), jnp.bfloat16)
    total[...] = jnp.zeros_like(total)
    table_copy.wait()

    for event in BEFORE:
        perform(event)
    for copy in tile_copies:
        copy.wait()

    def step(k, carry):
        for at, events in STEPS.items():
            @pl.when(k == at)
            def _():
                for event in events:
                    perform(event)
        column = panel_of[k] * NEED
        block = parts[k].reshape(NEED * TILE, TILE)
        for r in range(TPP):
            row = jnp.concatenate([tile_mem[table[r, column + s]] for s in range(NEED)], axis=1)
            total[r * TILE:(r + 1) * TILE, :] += jnp.dot(row, block, preferred_element_type=jnp.float32)
        return carry

    lax.fori_loop(0, TPP, step, 0)

    share_rows = TPP * TILE // FEAT
    order = [4, 5, 3, 2, 6, 7, 1]

    def mail_copy(step):
        to = (member + step) % FEAT
        return pltpu.make_async_remote_copy(
            src_ref=mail.at[to], dst_ref=inbox.at[member], send_sem=mail_send.at[step - 1], recv_sem=mail_recv.at[step - 1],
            device_id=(group, to), device_id_type=MESH)

    for n in order:
        to = (member + n) % FEAT
        mail[to] = total[pl.ds(pl.multiple_of(to * share_rows, share_rows), share_rows), :].astype(jnp.bfloat16)
        mail_copy(n).start()
    inbox[member] = total[pl.ds(pl.multiple_of(member * share_rows, share_rows), share_rows), :].astype(jnp.bfloat16)
    weight_copy.wait()
    for n in order:
        mail_copy(n).wait_recv()
    rows = jnp.concatenate([inbox[j] for j in range(FEAT)], axis=1)
    width = 256
    for c in range(out.shape[1] // width):
        cols = slice(c * width, (c + 1) * width)
        mixed = jnp.dot(rows, weight_mem[:, cols], preferred_element_type=jnp.float32)
        out[:, cols] = jnp.maximum(mixed, 0.0).astype(out.dtype)
    for w in INNER_LIST:
        for c in range(CHUNKS):
            inner_copy(w, c).wait_send()
    for w in LEAF_LIST:
        leaf_copy(w).wait_send()
    for n in order:
        mail_copy(n).wait_send()


def per_device(features, tiles, tile_row, tile_panel, tile_slot, counts, need_list, weight):
    width = features.shape[1]
    hidden = weight.shape[1]
    share_rows = TPP * TILE // FEAT
    any_spec = pl.BlockSpec(memory_space=pl.ANY)
    bf16 = jnp.bfloat16
    dma = pltpu.SemaphoreType.DMA
    return pl.pallas_call(
        layer_kernel,
        out_shape=jax.ShapeDtypeStruct((share_rows, hidden), bf16),
        in_specs=[any_spec] * 8,
        out_specs=pl.BlockSpec(memory_space=pltpu.VMEM),
        scratch_shapes=[pltpu.VMEM((TPP, TILE, width), bf16)] * 6 + [
            pltpu.VMEM((GROUPS, NEED, TILE, width), bf16),
            pltpu.VMEM((len(LEAF), NEED, TILE, width), bf16),
            pltpu.VMEM((MAXT + 1, TILE, TILE), bf16),
            pltpu.VMEM((TPP, TILE), jnp.int32),
            pltpu.SMEM((TPP, TILE), jnp.int32),
            pltpu.SMEM((MAXT,), jnp.int32),
            pltpu.SMEM((MAXT,), jnp.int32),
            pltpu.SMEM((MAXT,), jnp.int32),
            pltpu.SMEM((1,), jnp.int32),
            pltpu.SMEM((5, GROUPS, NEED), jnp.int32),
            pltpu.SMEM((GROUPS,), jnp.int32),
            pltpu.VMEM((TPP * TILE, width), jnp.float32),
            pltpu.VMEM((FEAT * width, hidden), bf16),
            pltpu.VMEM((FEAT, share_rows, width), bf16),
            pltpu.VMEM((FEAT, share_rows, width), bf16),
            dma((3,)), dma((TILE_DMAS,)), dma((9,)),
            dma((len(INNER) * CHUNKS,)), dma((len(INNER) * CHUNKS,)),
            dma((len(LEAF),)), dma((len(LEAF),)),
            dma((FEAT - 1,)), dma((FEAT - 1,)),
        ],
        compiler_params=pltpu.CompilerParams(collective_id=0, has_side_effects=True, vmem_limit_bytes=56 * 2**20),
        cost_estimate=pl.CostEstimate(flops=9 * 10**9, bytes_accessed=25 * 10**6, transcendentals=0),
    )(features.reshape(TPP, TILE, width), tiles, tile_row, tile_panel, tile_slot, counts, need_list, weight)


def solution(mesh):
    return jax.shard_map(
        per_device,
        mesh=mesh,
        in_specs=(P("rows", "feat"), P("rows", None, None), P("rows"), P("rows"), P("rows"), P("rows"), P(), P()),
        out_specs=P(("rows", "feat"), None),
        check_vma=False,
    )
```

```python
import functools

import jax
import jax.numpy as jnp
from jax import lax
from jax.experimental import pallas as pl
from jax.experimental.pallas import tpu as pltpu
from jax.sharding import PartitionSpec as P

TILE = 128
TPP = 16
NEED = 8
GROUPS = 16
FEAT = 8
MAXT = 640
CHUNKS = 4
PER = TPP // CHUNKS
TILE_DMAS = 8
MESH = pl.DeviceIdType.MESH

INNER = {4: (0, 2), 8: (0, 3), 6: (4, 1), 9: (8, 0), 11: (9, 1)}
LEAF = {1: (0, 0), 2: (0, 1), 10: (8, 1), 12: (8, 2), 5: (4, 0), 13: (9, 2), 7: (6, 0), 14: (6, 3), 3: (11, 3), 15: (11, 2)}
INNER_LIST = [4, 8, 6, 9, 11]
LEAF_LIST = list(LEAF)
HELD = [0] + INNER_LIST
ORDER = [0, 8, 4, 9, 6, 1, 12, 11, 2, 14, 5, 13, 7, 15, 3, 10]
CHILD = {4: [6], 8: [9], 9: [11]}

HALF = NEED // 2
SPLIT = 4
N_FULL = len(ORDER) - SPLIT

BEFORE = [
    ("in", 8, 0), ("in", 4, 0), ("in", 8, 1), ("in", 4, 1), ("in", 8, 2), ("in", 9, 0), ("in", 8, 3), ("in", 4, 2),
]
STEPS = {
    0: [("use", 0)],
    1: [("use", 8), ("in", 9, 1)],
    2: [("in", 4, 3), ("in", 9, 2), ("use", 4), ("send", 1), ("send", 12)],
    3: [("in", 9, 3), ("use", 9)],
    4: [("in", 6, 0), ("in", 6, 1), ("in", 6, 2), ("in", 6, 3), ("use", 6), ("send", 2), ("send", 14), ("send", 5), ("send", 13)],
    5: [("get", 1)],
    6: [("get", 12)],
    7: [("in", 11, 0), ("in", 11, 1), ("in", 11, 2), ("in", 11, 3), ("use", 11), ("send", 7), ("send", 15), ("send", 3), ("send", 10)],
    8: [("get", 2)],
    9: [("get", 14)],
    10: [("get", 5)],
    11: [("get", 13)],
}


def flip(c, bits):
    return (c, c + 1 - 2 * (c % 2), 3 - c, (c + 2) % 4)[bits]


def layer_kernel(features, tiles, row_hbm, panel_hbm, slot_hbm, count_hbm, need_hbm, weight, out,
                 held0, held1, held2, held3, held4, held5, parts, outbox, tile_mem, table_vec, table, row_mem, panel_mem,
                 slot_mem, count_mem, need_mem, panel_of, total, weight_mem, mail, inbox, mixed,
                 local_sem, tile_sem, small_sem, inner_send, inner_recv, leaf_send, leaf_recv, mail_send, mail_recv):
    group, member = lax.axis_index("rows"), lax.axis_index("feat")
    core = member % 2
    y, z = group // 4, group % 4
    first, second = y + core * (z - y), z + core * (y - z)
    held = dict(zip(HELD, (held0, held1, held2, held3, held4, held5)))

    def group_at(v):
        a, b = flip(first, v & 3), flip(second, v >> 2)
        return (a + core * (b - a)) * 4 + b + core * (a - b)

    own_copy = pltpu.make_async_copy(features, held0, local_sem.at[0])
    own_copy.start()
    small = [
        pltpu.make_async_copy(row_hbm, row_mem, small_sem.at[0]),
        pltpu.make_async_copy(panel_hbm, panel_mem, small_sem.at[1]),
        pltpu.make_async_copy(slot_hbm, slot_mem, small_sem.at[2]),
        pltpu.make_async_copy(count_hbm, count_mem, small_sem.at[3]),
        pltpu.make_async_copy(need_hbm.at[group], need_mem.at[0], small_sem.at[4]),
    ] + [
        pltpu.make_async_copy(need_hbm.at[group_at(1 << d)], need_mem.at[1 + d], small_sem.at[5 + d]) for d in range(4)
    ]
    for copy in small:
        copy.start()

    barrier = pltpu.get_barrier_semaphore()
    for d in range(4):
        pl.semaphore_signal(barrier, inc=1, device_id=(group_at(1 << d), member), device_id_type=MESH)
    for step in range(1, FEAT):
        pl.semaphore_signal(barrier, inc=1, device_id=(group, (member + step) % FEAT), device_id_type=MESH)

    share = MAXT // TILE_DMAS
    tile_copies = [
        pltpu.make_async_copy(tiles.at[pl.ds(i * share, share)], tile_mem.at[pl.ds(i * share, share)], tile_sem.at[i])
        for i in range(TILE_DMAS)
    ]
    weight_copy = pltpu.make_async_copy(weight, weight_mem, local_sem.at[1])
    for copy in tile_copies + [weight_copy]:
        copy.start()

    def inner_copy(w, c):
        v, d = INNER[w]
        i = INNER_LIST.index(w) * CHUNKS + c
        rows = pl.ds(c * PER, PER)
        return pltpu.make_async_remote_copy(
            src_ref=held[v].at[rows], dst_ref=held[w].at[rows], send_sem=inner_send.at[i], recv_sem=inner_recv.at[i],
            device_id=(group_at(1 << d), member), device_id_type=MESH)

    def leaf_copy(w, part):
        d = LEAF[w][1]
        i = LEAF_LIST.index(w)
        blocks = pl.ds(part * HALF, HALF)
        return pltpu.make_async_remote_copy(
            src_ref=outbox.at[i, blocks], dst_ref=parts.at[ORDER.index(w), blocks], send_sem=leaf_send.at[2 * i + part],
            recv_sem=leaf_recv.at[2 * i + part],
            device_id=(group_at(1 << d), member), device_id_type=MESH)

    def perform(event):
        kind, v = event[0], event[1]
        if kind == "in":
            inner_copy(v, event[2]).wait_recv()
            for w in CHILD.get(v, []):
                inner_copy(w, event[2]).start()
        elif kind == "use":
            k, panel = ORDER.index(v), group_at(v)
            for s in range(NEED):
                parts[k, s] = held[v][need_mem[0, s, panel]]
        elif kind == "send":
            u, d = LEAF[v]
            i, panel = LEAF_LIST.index(v), group_at(u)
            for s in range(NEED):
                outbox[i, s] = held[u][need_mem[1 + d, s, panel]]
            for part in range(2):
                leaf_copy(v, part).start()
        else:
            for part in range(2):
                leaf_copy(v, part).wait_recv()

    own_copy.wait()
    pl.semaphore_wait(barrier, 4 + FEAT - 1)
    for c in range(CHUNKS):
        inner_copy(8, c).start()
        inner_copy(4, c).start()
    for copy in small:
        copy.wait()

    for k, v in enumerate(ORDER):
        panel_of[k] = group_at(v)
    count = count_mem[0]
    place = lax.broadcasted_iota(jnp.int32, (TPP, TILE), 0) * TILE + lax.broadcasted_iota(jnp.int32, (TPP, TILE), 1)

    def enter(k, found):
        code = row_mem[k] * TILE + panel_mem[k] * NEED + slot_mem[k]
        code = jnp.where(k < count, code, -1)
        return jnp.where(place == code, k, found)

    table_vec[...] = lax.fori_loop(0, MAXT, enter, jnp.full((TPP, TILE), MAXT, jnp.int32), unroll=8)
    table_copy = pltpu.make_async_copy(table_vec, table, local_sem.at[2])
    table_copy.start()
    tile_mem[MAXT] = jnp.zeros((TILE, TILE), jnp.bfloat16)
    total[...] = jnp.zeros_like(total)
    table_copy.wait()

    for event in BEFORE:
        perform(event)
    for copy in tile_copies:
        copy.wait()

    def step(k, carry):
        for at, events in STEPS.items():
            @pl.when(k == at)
            def _():
                for event in events:
                    perform(event)
        column = panel_of[k] * NEED
        block = parts[k].reshape(NEED * TILE, TILE)
        for r in range(TPP):
            row = jnp.concatenate([tile_mem[table[r, column + s]] for s in range(NEED)], axis=1)
            total[r * TILE:(r + 1) * TILE, :] += jnp.dot(row, block, preferred_element_type=jnp.float32)
        return carry

    lax.fori_loop(0, N_FULL, step, 0)

    def early(t, carry):
        for at in range(SPLIT):
            @pl.when(t == at)
            def _():
                leaf_copy(ORDER[N_FULL + at], 0).wait_recv()
        k = N_FULL + t
        column = panel_of[k] * NEED
        block = parts[k, :HALF].reshape(HALF * TILE, TILE)
        for r in range(TPP):
            row = jnp.concatenate([tile_mem[table[r, column + s]] for s in range(HALF)], axis=1)
            total[r * TILE:(r + 1) * TILE, :] += jnp.dot(row, block, preferred_element_type=jnp.float32)
        return carry

    lax.fori_loop(0, SPLIT, early, 0)

    for v in ORDER[N_FULL:]:
        leaf_copy(v, 1).wait_recv()
    share_rows = TPP * TILE // FEAT
    chip, chips = member // 2, FEAT // 2

    def mail_place(step, other):
        return (chip + step) % chips * 2 + core + other * (1 - 2 * core)

    def mail_copy(step, other):
        to = mail_place(step, other)
        return pltpu.make_async_remote_copy(
            src_ref=mail.at[to], dst_ref=inbox.at[member], send_sem=mail_send.at[step * 2 + other],
            recv_sem=mail_recv.at[step * 2 + other], device_id=(group, to), device_id_type=MESH)

    mail_order = [(2, 0), (2, 1), (1, 0), (3, 0), (1, 1), (3, 1), (0, 1), (0, 0)]
    columns = [panel_of[k] * NEED + HALF for k in range(N_FULL, len(ORDER))]
    block = jnp.concatenate([parts[k, HALF:].reshape(HALF * TILE, TILE) for k in range(N_FULL, len(ORDER))], axis=0)
    for step, other in mail_order:
        to = mail_place(step, other)
        for q in range(2):
            row = jnp.concatenate([tile_mem[table[to * 2 + q, column + s]] for column in columns for s in range(HALF)], axis=1)
            rows = pl.ds(pl.multiple_of((to * 2 + q) * TILE, TILE), TILE)
            done = total[rows, :] + jnp.dot(row, block, preferred_element_type=jnp.float32)
            place_rows = pl.ds(q * TILE, TILE)
            if (step, other) == (0, 0):
                inbox[to, place_rows, :] = done.astype(jnp.bfloat16)
            else:
                mail[to, place_rows, :] = done.astype(jnp.bfloat16)
        if (step, other) != (0, 0):
            mail_copy(step, other).start()

    weight_copy.wait()
    width = 256
    arrivals = [0, 2, 3, 1]
    for n, away in enumerate(arrivals):
        back = (chips - away) % chips
        for other in range(2):
            if (back, other) != (0, 0):
                mail_copy(back, other).wait_recv()
        source = (chip + away) % chips
        rows = jnp.concatenate([inbox[source * 2], inbox[source * 2 + 1]], axis=1)
        depth = pl.ds(pl.multiple_of(source * 2 * TILE, 2 * TILE), 2 * TILE)
        for c in range(out.shape[1] // width):
            cols = slice(c * width, (c + 1) * width)
            product = jnp.dot(rows, weight_mem[depth, cols], preferred_element_type=jnp.float32)
            if n > 0:
                product = product + mixed[:, cols]
            if n < chips - 1:
                mixed[:, cols] = product
            else:
                out[:, cols] = jnp.maximum(product, 0.0).astype(out.dtype)
    for w in INNER_LIST:
        for c in range(CHUNKS):
            inner_copy(w, c).wait_send()
    for w in LEAF_LIST:
        for part in range(2):
            leaf_copy(w, part).wait_send()
    for step, other in mail_order[:-1]:
        mail_copy(step, other).wait_send()


def per_device(features, tiles, tile_row, tile_panel, tile_slot, counts, need_list, weight):
    width = features.shape[1]
    hidden = weight.shape[1]
    share_rows = TPP * TILE // FEAT
    any_spec = pl.BlockSpec(memory_space=pl.ANY)
    bf16 = jnp.bfloat16
    dma = pltpu.SemaphoreType.DMA
    return pl.pallas_call(
        layer_kernel,
        out_shape=jax.ShapeDtypeStruct((share_rows, hidden), bf16),
        in_specs=[any_spec] * 8,
        out_specs=pl.BlockSpec(memory_space=pltpu.VMEM),
        scratch_shapes=[pltpu.VMEM((TPP, TILE, width), bf16)] * 6 + [
            pltpu.VMEM((GROUPS, NEED, TILE, width), bf16),
            pltpu.VMEM((len(LEAF), NEED, TILE, width), bf16),
            pltpu.VMEM((MAXT + 1, TILE, TILE), bf16),
            pltpu.VMEM((TPP, TILE), jnp.int32),
            pltpu.SMEM((TPP, TILE), jnp.int32),
            pltpu.SMEM((MAXT,), jnp.int32),
            pltpu.SMEM((MAXT,), jnp.int32),
            pltpu.SMEM((MAXT,), jnp.int32),
            pltpu.SMEM((1,), jnp.int32),
            pltpu.SMEM((5, NEED, GROUPS), jnp.int32),
            pltpu.SMEM((GROUPS,), jnp.int32),
            pltpu.VMEM((TPP * TILE, width), jnp.float32),
            pltpu.VMEM((FEAT * width, hidden), bf16),
            pltpu.VMEM((FEAT, share_rows, width), bf16),
            pltpu.VMEM((FEAT, share_rows, width), bf16),
            pltpu.VMEM((share_rows, hidden), jnp.float32),
            dma((3,)), dma((TILE_DMAS,)), dma((9,)),
            dma((len(INNER) * CHUNKS,)), dma((len(INNER) * CHUNKS,)),
            dma((2 * len(LEAF),)), dma((2 * len(LEAF),)),
            dma((FEAT,)), dma((FEAT,)),
        ],
        compiler_params=pltpu.CompilerParams(collective_id=0, has_side_effects=True, vmem_limit_bytes=56 * 2**20),
        cost_estimate=pl.CostEstimate(flops=9 * 10**9, bytes_accessed=25 * 10**6, transcendentals=0),
    )(features.reshape(TPP, TILE, width), tiles, tile_row, tile_panel, tile_slot, counts, need_list.transpose(0, 2, 1), weight)


def solution(mesh):
    return jax.shard_map(
        per_device,
        mesh=mesh,
        in_specs=(P("rows", "feat"), P("rows", None, None), P("rows"), P("rows"), P("rows"), P("rows"), P(), P()),
        out_specs=P(("rows", "feat"), None),
        check_vma=False,
    )
```

```python
import functools

import jax
import jax.numpy as jnp
from jax import lax
from jax.experimental import pallas as pl
from jax.experimental.pallas import tpu as pltpu
from jax.sharding import PartitionSpec as P

TILE = 128
TPP = 16
NEED = 8
GROUPS = 16
FEAT = 8
MAXT = 640
CHUNKS = 4
PER = TPP // CHUNKS
TILE_DMAS = 8
MESH = pl.DeviceIdType.MESH

INNER = {4: (0, 2), 8: (0, 3), 6: (4, 1), 9: (8, 0), 11: (9, 1)}
LEAF = {1: (0, 0), 2: (0, 1), 10: (8, 1), 12: (8, 2), 5: (4, 0), 13: (9, 2), 7: (6, 0), 14: (6, 3), 3: (11, 3), 15: (11, 2)}
INNER_LIST = [4, 8, 6, 9, 11]
LEAF_LIST = list(LEAF)
HELD = [0] + INNER_LIST
ORDER = [0, 8, 4, 9, 6, 1, 12, 11, 2, 14, 5, 13, 7, 15, 3, 10]
CHILD = {4: [6], 8: [9], 9: [11]}

HALF = NEED // 2
SPLIT = 4
N_FULL = len(ORDER) - SPLIT

BEFORE = [
    ("in", 8, 0), ("in", 4, 0), ("in", 8, 1), ("in", 4, 1), ("in", 8, 2), ("in", 9, 0), ("in", 8, 3), ("in", 4, 2),
]
STEPS = {
    0: [("use", 0)],
    1: [("use", 8), ("in", 9, 1)],
    2: [("in", 4, 3), ("in", 9, 2), ("use", 4), ("send", 1), ("send", 12)],
    3: [("in", 9, 3), ("use", 9)],
    4: [("in", 6, 0), ("in", 6, 1), ("in", 6, 2), ("in", 6, 3), ("use", 6), ("send", 2), ("send", 14), ("send", 5), ("send", 13)],
    5: [("get", 1)],
    6: [("get", 12)],
    7: [("in", 11, 0), ("in", 11, 1), ("in", 11, 2), ("in", 11, 3), ("use", 11), ("send", 7), ("send", 15), ("send", 3), ("send", 10)],
    8: [("get", 2)],
    9: [("get", 14)],
    10: [("get", 5)],
    11: [("get", 13)],
}


def flip(c, bits):
    return (c, c + 1 - 2 * (c % 2), 3 - c, (c + 2) % 4)[bits]


def layer_kernel(features, tiles, row_hbm, panel_hbm, slot_hbm, count_hbm, need_hbm, weight, out,
                 held0, held1, held2, held3, held4, held5, parts, outbox, tile_mem, table_vec, table, row_mem, panel_mem,
                 slot_mem, count_mem, need_mem, panel_of, total, weight_mem, mail, inbox, mixed,
                 local_sem, tile_sem, small_sem, inner_send, inner_recv, leaf_send, leaf_recv, mail_send, mail_recv):
    group, member = lax.axis_index("rows"), lax.axis_index("feat")
    core = member % 2
    y, z = group // 4, group % 4
    first, second = y + core * (z - y), z + core * (y - z)
    held = dict(zip(HELD, (held0, held1, held2, held3, held4, held5)))

    def group_at(v):
        a, b = flip(first, v & 3), flip(second, v >> 2)
        return (a + core * (b - a)) * 4 + b + core * (a - b)

    barrier = pltpu.get_barrier_semaphore()
    for d in range(4):
        pl.semaphore_signal(barrier, inc=1, device_id=(group_at(1 << d), member), device_id_type=MESH)
    for step in range(1, FEAT):
        pl.semaphore_signal(barrier, inc=1, device_id=(group, (member + step) % FEAT), device_id_type=MESH)

    own_copy = pltpu.make_async_copy(features, held0, local_sem.at[0])
    own_copy.start()
    small = [
        pltpu.make_async_copy(row_hbm, row_mem, small_sem.at[0]),
        pltpu.make_async_copy(panel_hbm, panel_mem, small_sem.at[1]),
        pltpu.make_async_copy(slot_hbm, slot_mem, small_sem.at[2]),
        pltpu.make_async_copy(count_hbm, count_mem, small_sem.at[3]),
        pltpu.make_async_copy(need_hbm.at[group], need_mem.at[0], small_sem.at[4]),
    ] + [
        pltpu.make_async_copy(need_hbm.at[group_at(1 << d)], need_mem.at[1 + d], small_sem.at[5 + d]) for d in range(4)
    ]
    for copy in small:
        copy.start()

    share = MAXT // TILE_DMAS
    tile_copies = [
        pltpu.make_async_copy(tiles.at[pl.ds(i * share, share)], tile_mem.at[pl.ds(i * share, share)], tile_sem.at[i])
        for i in range(TILE_DMAS)
    ]
    weight_copy = pltpu.make_async_copy(weight, weight_mem, local_sem.at[1])
    for copy in tile_copies + [weight_copy]:
        copy.start()

    def inner_copy(w, c):
        v, d = INNER[w]
        i = INNER_LIST.index(w) * CHUNKS + c
        rows = pl.ds(c * PER, PER)
        return pltpu.make_async_remote_copy(
            src_ref=(held[v] if v else features).at[rows], dst_ref=held[w].at[rows], send_sem=inner_send.at[i], recv_sem=inner_recv.at[i],
            device_id=(group_at(1 << d), member), device_id_type=MESH)

    def leaf_copy(w, part):
        d = LEAF[w][1]
        i = LEAF_LIST.index(w)
        blocks = pl.ds(part * HALF, HALF)
        return pltpu.make_async_remote_copy(
            src_ref=outbox.at[i, blocks], dst_ref=parts.at[ORDER.index(w), blocks], send_sem=leaf_send.at[2 * i + part],
            recv_sem=leaf_recv.at[2 * i + part],
            device_id=(group_at(1 << d), member), device_id_type=MESH)

    def perform(event):
        kind, v = event[0], event[1]
        if kind == "in":
            inner_copy(v, event[2]).wait_recv()
            for w in CHILD.get(v, []):
                inner_copy(w, event[2]).start()
        elif kind == "use":
            k, panel = ORDER.index(v), group_at(v)
            for s in range(NEED):
                parts[k, s] = held[v][need_mem[0, s, panel]]
        elif kind == "send":
            u, d = LEAF[v]
            i, panel = LEAF_LIST.index(v), group_at(u)
            for s in range(NEED):
                outbox[i, s] = held[u][need_mem[1 + d, s, panel]]
            for part in range(2):
                leaf_copy(v, part).start()
        else:
            for part in range(2):
                leaf_copy(v, part).wait_recv()

    pl.semaphore_wait(barrier, 4 + FEAT - 1)
    for c in range(CHUNKS):
        inner_copy(8, c).start()
        inner_copy(4, c).start()
    for copy in small:
        copy.wait()
    own_copy.wait()

    for k, v in enumerate(ORDER):
        panel_of[k] = group_at(v)
    count = count_mem[0]
    place = lax.broadcasted_iota(jnp.int32, (TPP, TILE), 0) * TILE + lax.broadcasted_iota(jnp.int32, (TPP, TILE), 1)

    def enter(k, found):
        code = row_mem[k] * TILE + panel_mem[k] * NEED + slot_mem[k]
        code = jnp.where(k < count, code, -1)
        return jnp.where(place == code, k, found)

    table_vec[...] = lax.fori_loop(0, MAXT, enter, jnp.full((TPP, TILE), MAXT, jnp.int32), unroll=8)
    table_copy = pltpu.make_async_copy(table_vec, table, local_sem.at[2])
    table_copy.start()
    tile_mem[MAXT] = jnp.zeros((TILE, TILE), jnp.bfloat16)
    total[...] = jnp.zeros_like(total)
    table_copy.wait()

    for event in BEFORE:
        perform(event)
    for copy in tile_copies:
        copy.wait()

    def step(k, carry):
        for at, events in STEPS.items():
            @pl.when(k == at)
            def _():
                for event in events:
                    perform(event)
        column = panel_of[k] * NEED
        block = parts[k].reshape(NEED * TILE, TILE)
        for r in range(TPP):
            row = jnp.concatenate([tile_mem[table[r, column + s]] for s in range(NEED)], axis=1)
            total[r * TILE:(r + 1) * TILE, :] += jnp.dot(row, block, preferred_element_type=jnp.float32)
        return carry

    lax.fori_loop(0, N_FULL, step, 0)

    def early(t, carry):
        for at in range(SPLIT):
            @pl.when(t == at)
            def _():
                leaf_copy(ORDER[N_FULL + at], 0).wait_recv()
        k = N_FULL + t
        column = panel_of[k] * NEED
        block = parts[k, :HALF].reshape(HALF * TILE, TILE)
        for r in range(TPP):
            row = jnp.concatenate([tile_mem[table[r, column + s]] for s in range(HALF)], axis=1)
            total[r * TILE:(r + 1) * TILE, :] += jnp.dot(row, block, preferred_element_type=jnp.float32)
        return carry

    lax.fori_loop(0, SPLIT, early, 0)

    for v in ORDER[N_FULL:]:
        leaf_copy(v, 1).wait_recv()
    share_rows = TPP * TILE // FEAT
    chip, chips = member // 2, FEAT // 2

    def mail_place(step, other):
        return (chip + step) % chips * 2 + core + other * (1 - 2 * core)

    def mail_copy(step, other):
        to = mail_place(step, other)
        return pltpu.make_async_remote_copy(
            src_ref=mail.at[to], dst_ref=inbox.at[member], send_sem=mail_send.at[step * 2 + other],
            recv_sem=mail_recv.at[step * 2 + other], device_id=(group, to), device_id_type=MESH)

    mail_order = [(2, 0), (2, 1), (1, 0), (3, 0), (1, 1), (3, 1), (0, 1), (0, 0)]
    columns = [panel_of[k] * NEED + HALF for k in range(N_FULL, len(ORDER))]
    block = jnp.concatenate([parts[k, HALF:].reshape(HALF * TILE, TILE) for k in range(N_FULL, len(ORDER))], axis=0)
    for step, other in mail_order:
        to = mail_place(step, other)
        for q in range(2):
            row = jnp.concatenate([tile_mem[table[to * 2 + q, column + s]] for column in columns for s in range(HALF)], axis=1)
            rows = pl.ds(pl.multiple_of((to * 2 + q) * TILE, TILE), TILE)
            done = total[rows, :] + jnp.dot(row, block, preferred_element_type=jnp.float32)
            place_rows = pl.ds(q * TILE, TILE)
            if (step, other) == (0, 0):
                inbox[to, place_rows, :] = done.astype(jnp.bfloat16)
            else:
                mail[to, place_rows, :] = done.astype(jnp.bfloat16)
        if (step, other) != (0, 0):
            mail_copy(step, other).start()

    weight_copy.wait()
    width = 256
    arrivals = [0, 2, 3, 1]
    for n, away in enumerate(arrivals):
        back = (chips - away) % chips
        for other in range(2):
            if (back, other) != (0, 0):
                mail_copy(back, other).wait_recv()
        source = (chip + away) % chips
        rows = jnp.concatenate([inbox[source * 2], inbox[source * 2 + 1]], axis=1)
        depth = pl.ds(pl.multiple_of(source * 2 * TILE, 2 * TILE), 2 * TILE)
        for c in range(out.shape[1] // width):
            cols = slice(c * width, (c + 1) * width)
            product = jnp.dot(rows, weight_mem[depth, cols], preferred_element_type=jnp.float32)
            if n > 0:
                product = product + mixed[:, cols]
            if n < chips - 1:
                mixed[:, cols] = product
            else:
                out[:, cols] = jnp.maximum(product, 0.0).astype(out.dtype)
    for w in INNER_LIST:
        for c in range(CHUNKS):
            inner_copy(w, c).wait_send()
    for w in LEAF_LIST:
        for part in range(2):
            leaf_copy(w, part).wait_send()
    for step, other in mail_order[:-1]:
        mail_copy(step, other).wait_send()


def per_device(features, tiles, tile_row, tile_panel, tile_slot, counts, need_list, weight):
    width = features.shape[1]
    hidden = weight.shape[1]
    share_rows = TPP * TILE // FEAT
    any_spec = pl.BlockSpec(memory_space=pl.ANY)
    bf16 = jnp.bfloat16
    dma = pltpu.SemaphoreType.DMA
    return pl.pallas_call(
        layer_kernel,
        out_shape=jax.ShapeDtypeStruct((share_rows, hidden), bf16),
        in_specs=[any_spec] * 8,
        out_specs=pl.BlockSpec(memory_space=pltpu.VMEM),
        scratch_shapes=[pltpu.VMEM((TPP, TILE, width), bf16)] * 6 + [
            pltpu.VMEM((GROUPS, NEED, TILE, width), bf16),
            pltpu.VMEM((len(LEAF), NEED, TILE, width), bf16),
            pltpu.VMEM((MAXT + 1, TILE, TILE), bf16),
            pltpu.VMEM((TPP, TILE), jnp.int32),
            pltpu.SMEM((TPP, TILE), jnp.int32),
            pltpu.SMEM((MAXT,), jnp.int32),
            pltpu.SMEM((MAXT,), jnp.int32),
            pltpu.SMEM((MAXT,), jnp.int32),
            pltpu.SMEM((1,), jnp.int32),
            pltpu.SMEM((5, NEED, GROUPS), jnp.int32),
            pltpu.SMEM((GROUPS,), jnp.int32),
            pltpu.VMEM((TPP * TILE, width), jnp.float32),
            pltpu.VMEM((FEAT * width, hidden), bf16),
            pltpu.VMEM((FEAT, share_rows, width), bf16),
            pltpu.VMEM((FEAT, share_rows, width), bf16),
            pltpu.VMEM((share_rows, hidden), jnp.float32),
            dma((3,)), dma((TILE_DMAS,)), dma((9,)),
            dma((len(INNER) * CHUNKS,)), dma((len(INNER) * CHUNKS,)),
            dma((2 * len(LEAF),)), dma((2 * len(LEAF),)),
            dma((FEAT,)), dma((FEAT,)),
        ],
        compiler_params=pltpu.CompilerParams(collective_id=0, has_side_effects=True, vmem_limit_bytes=56 * 2**20),
        cost_estimate=pl.CostEstimate(flops=9 * 10**9, bytes_accessed=25 * 10**6, transcendentals=0),
    )(features.reshape(TPP, TILE, width), tiles, tile_row, tile_panel, tile_slot, counts, need_list.transpose(0, 2, 1), weight)


def solution(mesh):
    return jax.shard_map(
        per_device,
        mesh=mesh,
        in_specs=(P("rows", "feat"), P("rows", None, None), P("rows"), P("rows"), P("rows"), P("rows"), P(), P()),
        out_specs=P(("rows", "feat"), None),
        check_vma=False,
    )
```

```python
import functools

import jax
import jax.numpy as jnp
from jax import lax
from jax.experimental import pallas as pl
from jax.experimental.pallas import tpu as pltpu
from jax.sharding import PartitionSpec as P

TILE = 128
TPP = 16
NEED = 8
GROUPS = 16
FEAT = 8
MAXT = 640
CHUNKS = 4
PER = TPP // CHUNKS
TILE_DMAS = 8
MESH = pl.DeviceIdType.MESH

INNER = {4: (0, 2), 8: (0, 3), 6: (4, 1), 9: (8, 0), 11: (9, 1)}
LEAF = {1: (0, 0), 2: (0, 1), 10: (8, 1), 12: (8, 2), 5: (4, 0), 13: (9, 2), 7: (6, 0), 14: (6, 3), 3: (11, 3), 15: (11, 2)}
INNER_LIST = [4, 8, 6, 9, 11]
LEAF_LIST = list(LEAF)
HELD = [0] + INNER_LIST
ORDER = [0, 8, 4, 9, 6, 1, 12, 11, 2, 14, 5, 13, 7, 15, 3, 10]
CHILD = {4: [6], 8: [9], 9: [11]}

HALF = NEED // 2
SPLIT = 4
N_FULL = len(ORDER) - SPLIT

BEFORE = [
    ("in", 8, 0), ("in", 4, 0), ("in", 8, 1), ("in", 4, 1), ("in", 8, 2), ("in", 9, 0), ("in", 8, 3), ("in", 4, 2),
]
STEPS = {
    0: [("use", 0)],
    1: [("use", 8), ("in", 9, 1)],
    2: [("in", 4, 3), ("in", 9, 2), ("use", 4), ("send", 1), ("send", 12)],
    3: [("in", 9, 3), ("use", 9), ("send", 5), ("send", 13)],
    4: [("in", 6, 0), ("in", 6, 1), ("in", 6, 2), ("in", 6, 3), ("use", 6), ("send", 2), ("send", 14), ("send", 7)],
    5: [("get", 1)],
    6: [("get", 12)],
    7: [("in", 11, 0), ("in", 11, 1), ("in", 11, 2), ("in", 11, 3), ("use", 11), ("send", 15), ("send", 3), ("send", 10)],
    8: [("get", 2)],
    9: [("get", 14)],
    10: [("get", 5)],
    11: [("get", 13)],
}


def flip(c, bits):
    return (c, c + 1 - 2 * (c % 2), 3 - c, (c + 2) % 4)[bits]


def layer_kernel(features, tiles, row_hbm, panel_hbm, slot_hbm, count_hbm, need_hbm, weight, out,
                 held0, held1, held2, held3, held4, held5, parts, outbox, tile_mem, table_vec, table, row_mem, panel_mem,
                 slot_mem, count_mem, need_mem, panel_of, total, weight_mem, mail, inbox, mixed,
                 local_sem, tile_sem, small_sem, inner_send, inner_recv, leaf_send, leaf_recv, mail_send, mail_recv):
    group, member = lax.axis_index("rows"), lax.axis_index("feat")
    core = member % 2
    y, z = group // 4, group % 4
    first, second = y + core * (z - y), z + core * (y - z)
    held = dict(zip(HELD, (held0, held1, held2, held3, held4, held5)))

    def group_at(v):
        a, b = flip(first, v & 3), flip(second, v >> 2)
        return (a + core * (b - a)) * 4 + b + core * (a - b)

    barrier = pltpu.get_barrier_semaphore()
    for d in range(4):
        pl.semaphore_signal(barrier, inc=1, device_id=(group_at(1 << d), member), device_id_type=MESH)
    for step in range(1, FEAT):
        pl.semaphore_signal(barrier, inc=1, device_id=(group, (member + step) % FEAT), device_id_type=MESH)

    own_copy = pltpu.make_async_copy(features, held0, local_sem.at[0])
    own_copy.start()
    small = [
        pltpu.make_async_copy(row_hbm, row_mem, small_sem.at[0]),
        pltpu.make_async_copy(panel_hbm, panel_mem, small_sem.at[1]),
        pltpu.make_async_copy(slot_hbm, slot_mem, small_sem.at[2]),
        pltpu.make_async_copy(count_hbm, count_mem, small_sem.at[3]),
        pltpu.make_async_copy(need_hbm.at[group], need_mem.at[0], small_sem.at[4]),
    ] + [
        pltpu.make_async_copy(need_hbm.at[group_at(1 << d)], need_mem.at[1 + d], small_sem.at[5 + d]) for d in range(4)
    ]
    for copy in small:
        copy.start()

    share = MAXT // TILE_DMAS
    tile_copies = [
        pltpu.make_async_copy(tiles.at[pl.ds(i * share, share)], tile_mem.at[pl.ds(i * share, share)], tile_sem.at[i])
        for i in range(TILE_DMAS)
    ]
    weight_copy = pltpu.make_async_copy(weight, weight_mem, local_sem.at[1])
    for copy in tile_copies + [weight_copy]:
        copy.start()

    def inner_copy(w, c):
        v, d = INNER[w]
        i = INNER_LIST.index(w) * CHUNKS + c
        rows = pl.ds(c * PER, PER)
        return pltpu.make_async_remote_copy(
            src_ref=(held[v] if v else features).at[rows], dst_ref=held[w].at[rows], send_sem=inner_send.at[i], recv_sem=inner_recv.at[i],
            device_id=(group_at(1 << d), member), device_id_type=MESH)

    def leaf_copy(w, part):
        d = LEAF[w][1]
        i = LEAF_LIST.index(w)
        blocks = pl.ds(part * HALF, HALF)
        return pltpu.make_async_remote_copy(
            src_ref=outbox.at[i, blocks], dst_ref=parts.at[ORDER.index(w), blocks], send_sem=leaf_send.at[2 * i + part],
            recv_sem=leaf_recv.at[2 * i + part],
            device_id=(group_at(1 << d), member), device_id_type=MESH)

    def perform(event):
        kind, v = event[0], event[1]
        if kind == "in":
            inner_copy(v, event[2]).wait_recv()
            for w in CHILD.get(v, []):
                inner_copy(w, event[2]).start()
        elif kind == "use":
            k, panel = ORDER.index(v), group_at(v)
            for s in range(NEED):
                parts[k, s] = held[v][need_mem[0, s, panel]]
        elif kind == "send":
            u, d = LEAF[v]
            i, panel = LEAF_LIST.index(v), group_at(u)
            for s in range(NEED):
                outbox[i, s] = held[u][need_mem[1 + d, s, panel]]
            for part in range(2):
                leaf_copy(v, part).start()
        else:
            for part in range(2):
                leaf_copy(v, part).wait_recv()

    pl.semaphore_wait(barrier, 4 + FEAT - 1)
    for c in range(CHUNKS):
        inner_copy(8, c).start()
        inner_copy(4, c).start()
    for copy in small:
        copy.wait()
    own_copy.wait()

    for k, v in enumerate(ORDER):
        panel_of[k] = group_at(v)
    count = count_mem[0]
    place = lax.broadcasted_iota(jnp.int32, (TPP, TILE), 0) * TILE + lax.broadcasted_iota(jnp.int32, (TPP, TILE), 1)

    def enter(k, found):
        code = row_mem[k] * TILE + panel_mem[k] * NEED + slot_mem[k]
        code = jnp.where(k < count, code, -1)
        return jnp.where(place == code, k, found)

    table_vec[...] = lax.fori_loop(0, MAXT, enter, jnp.full((TPP, TILE), MAXT, jnp.int32), unroll=8)
    table_copy = pltpu.make_async_copy(table_vec, table, local_sem.at[2])
    table_copy.start()
    tile_mem[MAXT] = jnp.zeros((TILE, TILE), jnp.bfloat16)
    total[...] = jnp.zeros_like(total)
    table_copy.wait()

    for event in BEFORE[:4]:
        perform(event)
    for copy in tile_copies:
        copy.wait()
    for event in BEFORE[4:]:
        perform(event)

    def step(k, carry):
        for at, events in STEPS.items():
            @pl.when(k == at)
            def _():
                for event in events:
                    perform(event)
        column = panel_of[k] * NEED
        block = parts[k].reshape(NEED * TILE, TILE)
        for r in range(TPP):
            row = jnp.concatenate([tile_mem[table[r, column + s]] for s in range(NEED)], axis=1)
            total[r * TILE:(r + 1) * TILE, :] += jnp.dot(row, block, preferred_element_type=jnp.float32)
        return carry

    lax.fori_loop(0, N_FULL, step, 0)

    def early(t, carry):
        for at in range(SPLIT):
            @pl.when(t == at)
            def _():
                leaf_copy(ORDER[N_FULL + at], 0).wait_recv()
        k = N_FULL + t
        column = panel_of[k] * NEED
        block = parts[k, :HALF].reshape(HALF * TILE, TILE)
        for r in range(TPP):
            row = jnp.concatenate([tile_mem[table[r, column + s]] for s in range(HALF)], axis=1)
            total[r * TILE:(r + 1) * TILE, :] += jnp.dot(row, block, preferred_element_type=jnp.float32)
        return carry

    lax.fori_loop(0, SPLIT, early, 0)

    for v in ORDER[N_FULL:]:
        leaf_copy(v, 1).wait_recv()
    share_rows = TPP * TILE // FEAT
    chip, chips = member // 2, FEAT // 2

    def mail_place(step, other):
        return (chip + step) % chips * 2 + core + other * (1 - 2 * core)

    def mail_copy(step, other):
        to = mail_place(step, other)
        return pltpu.make_async_remote_copy(
            src_ref=mail.at[to], dst_ref=inbox.at[member], send_sem=mail_send.at[step * 2 + other],
            recv_sem=mail_recv.at[step * 2 + other], device_id=(group, to), device_id_type=MESH)

    mail_order = [(2, 0), (2, 1), (1, 0), (3, 0), (1, 1), (3, 1), (0, 1), (0, 0)]
    columns = [panel_of[k] * NEED + HALF for k in range(N_FULL, len(ORDER))]
    block = jnp.concatenate([parts[k, HALF:].reshape(HALF * TILE, TILE) for k in range(N_FULL, len(ORDER))], axis=0)
    for step, other in mail_order:
        to = mail_place(step, other)
        for q in range(2):
            row = jnp.concatenate([tile_mem[table[to * 2 + q, column + s]] for column in columns for s in range(HALF)], axis=1)
            rows = pl.ds(pl.multiple_of((to * 2 + q) * TILE, TILE), TILE)
            done = total[rows, :] + jnp.dot(row, block, preferred_element_type=jnp.float32)
            place_rows = pl.ds(q * TILE, TILE)
            if (step, other) == (0, 0):
                inbox[to, place_rows, :] = done.astype(jnp.bfloat16)
            else:
                mail[to, place_rows, :] = done.astype(jnp.bfloat16)
        if (step, other) != (0, 0):
            mail_copy(step, other).start()

    weight_copy.wait()
    width = 256
    arrivals = [0, 2, 3, 1]
    for n, away in enumerate(arrivals):
        back = (chips - away) % chips
        for other in range(2):
            if (back, other) != (0, 0):
                mail_copy(back, other).wait_recv()
        source = (chip + away) % chips
        rows = jnp.concatenate([inbox[source * 2], inbox[source * 2 + 1]], axis=1)
        depth = pl.ds(pl.multiple_of(source * 2 * TILE, 2 * TILE), 2 * TILE)
        for c in range(out.shape[1] // width):
            cols = slice(c * width, (c + 1) * width)
            product = jnp.dot(rows, weight_mem[depth, cols], preferred_element_type=jnp.float32)
            if n > 0:
                product = product + mixed[:, cols]
            if n < chips - 1:
                mixed[:, cols] = product
            else:
                out[:, cols] = jnp.maximum(product, 0.0).astype(out.dtype)
    for w in INNER_LIST:
        for c in range(CHUNKS):
            inner_copy(w, c).wait_send()
    for w in LEAF_LIST:
        for part in range(2):
            leaf_copy(w, part).wait_send()
    for step, other in mail_order[:-1]:
        mail_copy(step, other).wait_send()


def per_device(features, tiles, tile_row, tile_panel, tile_slot, counts, need_list, weight):
    width = features.shape[1]
    hidden = weight.shape[1]
    share_rows = TPP * TILE // FEAT
    any_spec = pl.BlockSpec(memory_space=pl.ANY)
    bf16 = jnp.bfloat16
    dma = pltpu.SemaphoreType.DMA
    return pl.pallas_call(
        layer_kernel,
        out_shape=jax.ShapeDtypeStruct((share_rows, hidden), bf16),
        in_specs=[any_spec] * 8,
        out_specs=pl.BlockSpec(memory_space=pltpu.VMEM),
        scratch_shapes=[pltpu.VMEM((TPP, TILE, width), bf16)] * 6 + [
            pltpu.VMEM((GROUPS, NEED, TILE, width), bf16),
            pltpu.VMEM((len(LEAF), NEED, TILE, width), bf16),
            pltpu.VMEM((MAXT + 1, TILE, TILE), bf16),
            pltpu.VMEM((TPP, TILE), jnp.int32),
            pltpu.SMEM((TPP, TILE), jnp.int32),
            pltpu.SMEM((MAXT,), jnp.int32),
            pltpu.SMEM((MAXT,), jnp.int32),
            pltpu.SMEM((MAXT,), jnp.int32),
            pltpu.SMEM((1,), jnp.int32),
            pltpu.SMEM((5, NEED, GROUPS), jnp.int32),
            pltpu.SMEM((GROUPS,), jnp.int32),
            pltpu.VMEM((TPP * TILE, width), jnp.float32),
            pltpu.VMEM((FEAT * width, hidden), bf16),
            pltpu.VMEM((FEAT, share_rows, width), bf16),
            pltpu.VMEM((FEAT, share_rows, width), bf16),
            pltpu.VMEM((share_rows, hidden), jnp.float32),
            dma((3,)), dma((TILE_DMAS,)), dma((9,)),
            dma((len(INNER) * CHUNKS,)), dma((len(INNER) * CHUNKS,)),
            dma((2 * len(LEAF),)), dma((2 * len(LEAF),)),
            dma((FEAT,)), dma((FEAT,)),
        ],
        compiler_params=pltpu.CompilerParams(collective_id=0, has_side_effects=True, vmem_limit_bytes=56 * 2**20),
        cost_estimate=pl.CostEstimate(flops=9 * 10**9, bytes_accessed=25 * 10**6, transcendentals=0),
    )(features.reshape(TPP, TILE, width), tiles, tile_row, tile_panel, tile_slot, counts, need_list.transpose(0, 2, 1), weight)


def solution(mesh):
    return jax.shard_map(
        per_device,
        mesh=mesh,
        in_specs=(P("rows", "feat"), P("rows", None, None), P("rows"), P("rows"), P("rows"), P("rows"), P(), P()),
        out_specs=P(("rows", "feat"), None),
        check_vma=False,
    )
```
